32 devices in a mesh: groups: 2 (over y), tiles: 4 (over z), rep: 2 (over x), sub: 2 (over core).
Axes of the slice: x: 2, y: 2, z: 4, core: 2. Of those that a mesh axis runs over, the one named last changes fastest.
Arguments:
- amplitudes: float32 [8, 2, 6, 64, 1792], P(('groups', 'tiles'), 'rep'), parts along dimension 0, may hold values from -6 to 6
- integrals: float32 [16, 64, 2, 512], P(('groups', 'tiles'), 'sub', 'rep'), parts along dimension 0, may hold values from -0.21875 to 0.21875
- tile_owner: int32 [8, 2, 6], P(('groups', 'tiles'), 'rep'), parts along dimension 0, may hold values from 0 to 3, as said below
Outputs:
- cycle_term: float32 [16, 64, 1792], P(('groups', 'tiles', 'rep'), 'sub'), parts along dimension 0
The draws below stay inside these ranges and needn't reach their ends.
There are 2 independent parts, one for each index of `groups`. The reference program is written for one: setup_inputs(seed, part) draws one part's arguments, and reference() takes and returns one part's arrays. A program takes and returns all parts, laid end to end along the dimension named above; each array names one. Nothing has to cross between parts.
Inputs may be any that keep to these rules, and one draw needn't show every extreme that they name: `tile_owner`: within each storage block t, r no tiles index owns more than 2 tiles, and in every block one tiles index, the same for all blocks, owns exactly 2.
All inputs are finite; a program needn't handle non-finite values.
Results may differ from the reference program's by a relative error of at most 0.0003.
Values sent between devices are 32-bit elements; how exact they have to be, the bound alone decides.
No kernel may reach another device: no remote copies, remote signals or barrier semaphores. Data moves between devices by JAX's collectives and lax.ppermute only.
A program may use at most 128 MiB of HBM per device.

```python
import jax
import jax.numpy as jnp
from jax import lax

TILE = 64
CAP = 2
S_DEV = 6
COLS = 1792
NQ = 8
KW = 512
N_TILES = 4
N_REP = 2


def draw_tile_owner(key, part):
    key = jax.random.fold_in(key, 11)
    first_key, second_key, third_key = jax.random.split(key, 3)
    busiest = jax.random.randint(first_key, (), 0, N_TILES)
    destinations = jnp.arange(N_TILES * CAP, dtype=jnp.int32) // CAP
    block_keys = jax.random.split(second_key, N_TILES * N_REP)
    shuffled = jax.vmap(lambda one: jax.random.permutation(one, N_TILES * CAP))(block_keys).astype(jnp.int32)
    scores = jnp.where(destinations[None, :] == busiest, shuffled - N_TILES * CAP, shuffled)
    ordering = jnp.argsort(scores, axis=1, stable=True)[:, :S_DEV]
    chosen = destinations[ordering]
    mixing_keys = jax.random.split(third_key, N_TILES * N_REP)
    mixing = jax.vmap(lambda one: jax.random.permutation(one, S_DEV))(mixing_keys)
    placed = jnp.take_along_axis(chosen, mixing, axis=1)
    return placed.reshape(N_TILES, N_REP, S_DEV).astype(jnp.int32)


def shard_levels(own_key, extent, pieces, least, largest):
    gain = 1.0
    for dim, shards_of in pieces:
        heights = jax.random.uniform(jax.random.fold_in(jax.random.fold_in(own_key, 6), dim), (shards_of,), jnp.float32, least / len(pieces), largest / len(pieces))
        gain = gain * jnp.repeat(jnp.exp(heights), extent[dim] // shards_of).reshape((-1,) + (1,) * (len(extent) - 1 - dim))
    return gain


def normal_values(stream_key, shape, scale, bound, cuts=(), held_as=jnp.bfloat16):
    values = jax.random.normal(stream_key, shape, jnp.float32) * scale
    if len(cuts) > 0:
        values = shard_levels(stream_key, shape, cuts, -0.22, 0.18) * values
    return jnp.clip(values, min=-bound, max=bound).astype(held_as)


def setup_inputs(seed: int = 0, part: int = 0) -> dict:
    seeds = jax.random.split(jax.random.key(seed), 4)
    part_splits = jax.random.split(jax.random.fold_in(seeds[3], part), 4)
    return {
        "amplitudes": normal_values(part_splits[0], (N_TILES, N_REP, S_DEV, TILE, COLS), 1.0, 6.0, ((0, 4), (1, 2)), jnp.float32),
        "integrals": normal_values(part_splits[1], (NQ, TILE, N_REP, KW), (TILE * N_REP * S_DEV) ** -0.5, 0.21875, ((0, 4), (1, 2), (2, 2)), jnp.float32),
        "tile_owner": draw_tile_owner(jax.random.fold_in(jax.random.fold_in(seeds[3], part), 71), part),
    }


def rank_within(owners):
    length = owners.shape[-1]
    earlier = jnp.arange(length)[:, None] > jnp.arange(length)[None, :]
    matching = owners[..., :, None] == owners[..., None, :]
    return jnp.sum(matching & earlier, axis=-1).astype(jnp.int32)


def reference(amplitudes, integrals, tile_owner):
    ranking = rank_within(tile_owner)
    source = jnp.arange(N_TILES, dtype=jnp.int32)[:, None, None]
    slot_index = source * CAP + ranking
    rep_index = jnp.arange(N_REP, dtype=jnp.int32)[None, :, None] + jnp.zeros_like(slot_index)
    group_rows = NQ // N_TILES

    def one_group(group):
        target = jnp.where(tile_owner == group, slot_index, N_TILES * CAP).astype(jnp.int32)
        arrived = jnp.zeros((N_REP, N_TILES * CAP, TILE, COLS), jnp.float32)
        arrived = arrived.at[rep_index, target].set(amplitudes, mode="drop")
        arrived = arrived.reshape(N_REP, N_TILES * CAP * TILE, COLS)
        group_weights = lax.dynamic_slice_in_dim(integrals, (group * group_rows).astype(jnp.int32), group_rows, 0)
        return jnp.einsum("qbrk,rkc->qbc", group_weights, arrived, precision=lax.Precision.HIGHEST)

    result = lax.map(one_group, jnp.arange(N_TILES, dtype=jnp.int32))
    return result.reshape(NQ, TILE, COLS)
```

```python
import functools

import jax
import jax.numpy as jnp
from jax import lax
from jax.experimental import pallas as pl
from jax.experimental.pallas import tpu as pltpu
from jax.sharding import PartitionSpec as P

TILE = 64
CAP = 2
PAIR = TILE * CAP
VMEM_LIMIT = 32 * 1024 * 1024
ANY = pl.BlockSpec(memory_space=pl.ANY)
VMEM = pl.BlockSpec(memory_space=pltpu.VMEM)
SMEM = pl.BlockSpec(memory_space=pltpu.SMEM)


def f32(*shape):
    return jax.ShapeDtypeStruct(shape, jnp.float32)


def call(kernel, outs, ins, scratch=()):
    return functools.partial(
        pl.pallas_call,
        kernel,
        out_shape=outs,
        in_specs=ins,
        out_specs=jax.tree.map(lambda _: VMEM, outs),
        scratch_shapes=list(scratch),
        compiler_params=pltpu.CompilerParams(vmem_limit_bytes=VMEM_LIMIT),
        cost_estimate=pl.CostEstimate(flops=1, bytes_accessed=1, transcendentals=0),
    )()


def split(value):
    high = value.astype(jnp.bfloat16)
    low = (value - high.astype(jnp.float32)).astype(jnp.bfloat16)
    return high, low


def find(owner, target):
    found = []
    for slot in range(CAP):
        seen, index, filled = jnp.int32(0), jnp.int32(0), jnp.int32(0)
        for k in range(owner.shape[0]):
            match = owner[k] == target
            hit = jnp.logical_and(match, seen == slot)
            index = jnp.where(hit, k, index)
            filled = jnp.where(hit, 1, filled)
            seen = seen + match.astype(jnp.int32)
        found.append((index, filled))
    return found


def exchange(value, axis, distance):
    size = lax.axis_size(axis)
    return lax.ppermute(value, axis, [(i, i ^ distance) for i in range(size)])


def pick_kernel(integrals, *rest):
    *pieces, sems = rest
    here = lax.axis_index("tiles")
    copies = []
    for distance, piece in enumerate(pieces):
        start = pl.multiple_of((here ^ distance) * PAIR, PAIR)
        copies.append(pltpu.make_async_copy(integrals.at[:, pl.ds(start, PAIR)], piece, sems.at[distance]))
    for copy in copies:
        copy.start()
    for copy in copies:
        copy.wait()


def split_kernel(stored, high, low):
    value_high, value_low = split(stored[...])
    high[...] = value_high
    low[...] = value_low


def partial_kernel(distance, owner, piece, high, low, send, own):
    rows = own.shape[0]
    target = lax.axis_index("tiles") ^ distance
    rep = lax.axis_index("rep")
    (first, has_first), (second, has_second) = find(owner, target)
    lane = lax.broadcasted_iota(jnp.int32, (rows, PAIR), 1)
    kept = jnp.where(lane < TILE, has_first, has_second) == 1
    right_high = jnp.concatenate([high[first], high[second]], axis=0)
    right_low = jnp.concatenate([low[first], low[second]], axis=0)
    parts = []
    for pair_of in (1 - rep, rep):
        block = piece[pl.ds(pl.multiple_of(pair_of * rows, rows), rows), :]
        parts.append(jnp.where(kept, block, 0.0))
    left_high, left_low = split(jnp.concatenate(parts, axis=0))
    dot = functools.partial(jnp.dot, preferred_element_type=jnp.float32)
    product = dot(left_high, right_high) + (dot(left_high, right_low) + dot(left_low, right_high))
    send[...] = product[:rows]
    own[...] = product[rows:]


def square_shards(amplitudes, integrals, tile_owner):
    groups = lax.axis_size("tiles")
    stored = amplitudes.reshape(amplitudes.shape[2:])
    owner = tile_owner.reshape(tile_owner.shape[2])
    rows = integrals.shape[1]
    matrix = integrals.reshape(-1, integrals.shape[3])
    columns = stored.shape[2]

    picked = call(
        pick_kernel,
        [f32(matrix.shape[0], PAIR)] * groups,
        [ANY],
        [pltpu.SemaphoreType.DMA((groups,))],
    )(matrix)
    pieces = [picked[0]] + [exchange(picked[e], "tiles", e) for e in range(1, groups)]
    half = jax.ShapeDtypeStruct(stored.shape, jnp.bfloat16)
    high, low = pl.pallas_call(
        split_kernel,
        out_shape=[half, half],
        grid=(stored.shape[0],),
        in_specs=[pl.BlockSpec((1,) + stored.shape[1:], lambda k: (k, 0, 0))],
        out_specs=[pl.BlockSpec((1,) + stored.shape[1:], lambda k: (k, 0, 0))] * 2,
        compiler_params=pltpu.CompilerParams(vmem_limit_bytes=VMEM_LIMIT),
        cost_estimate=pl.CostEstimate(flops=1, bytes_accessed=1, transcendentals=0),
    )(stored)

    sums = {}
    for e in (2, 3, 1, 0):
        send, own = call(functools.partial(partial_kernel, e), [f32(rows, columns)] * 2, [SMEM] + [VMEM] * 3)(
            owner, pieces[e], high, low
        )
        sums[e] = own + exchange(send, "rep", 1)
    out = sums[0]
    for e in (2, 3, 1):
        out = out + exchange(sums[e], "tiles", e)
    return out.reshape(1, rows, columns)


def general_shards(amplitudes, integrals, tile_owner):
    tile_groups = lax.axis_size("tiles")
    stored = amplitudes.reshape(amplitudes.shape[2:])
    owners = tile_owner.reshape(tile_owner.shape[2])
    earlier = jnp.arange(owners.shape[0])[:, None] > jnp.arange(owners.shape[0])[None, :]
    matching = owners[:, None] == owners[None, :]
    slot_index = owners * CAP + jnp.sum(matching & earlier, axis=1)
    out_tiles, tile_rows, _, inner_width = integrals.shape
    columns = stored.shape[2]
    matrix = integrals.reshape(out_tiles * tile_rows, inner_width)
    outgoing = jnp.zeros((tile_groups * CAP, TILE, columns), jnp.float32).at[slot_index].set(stored)
    outgoing = outgoing.reshape(tile_groups, CAP, TILE, columns)
    received = lax.all_to_all(outgoing, "tiles", split_axis=0, concat_axis=0, tiled=True)
    product = jnp.dot(
        matrix, received.reshape(inner_width, columns), precision=lax.Precision.HIGHEST, preferred_element_type=jnp.float32
    )
    partial_value = product.reshape(out_tiles, tile_rows, columns)
    return lax.psum_scatter(partial_value, "rep", scatter_dimension=0, tiled=True)


def solution(mesh):
    small = mesh.shape["tiles"] == 4 and mesh.shape["rep"] == 2
    return jax.shard_map(
        square_shards if small else general_shards,
        mesh=mesh,
        in_specs=(
            P(("groups", "tiles"), "rep", None, None, None),
            P(("groups", "tiles"), "sub", "rep", None),
            P(("groups", "tiles"), "rep", None),
        ),
        out_specs=P(("groups", "tiles", "rep"), "sub", None),
        check_vma=False,
    )
```

```python
import functools

import jax
import jax.numpy as jnp
from jax import lax
from jax.experimental import pallas as pl
from jax.experimental.pallas import tpu as pltpu
from jax.sharding import PartitionSpec as P

TILE = 64
CAP = 2
PAIR = TILE * CAP
VMEM_LIMIT = 32 * 1024 * 1024
ANY = pl.BlockSpec(memory_space=pl.ANY)
VMEM = pl.BlockSpec(memory_space=pltpu.VMEM)
SMEM = pl.BlockSpec(memory_space=pltpu.SMEM)


def f32(*shape):
    return jax.ShapeDtypeStruct(shape, jnp.float32)


def call(kernel, outs, ins, scratch=(), flops=1):
    return functools.partial(
        pl.pallas_call,
        kernel,
        out_shape=outs,
        in_specs=ins,
        out_specs=jax.tree.map(lambda _: VMEM, outs),
        scratch_shapes=list(scratch),
        compiler_params=pltpu.CompilerParams(vmem_limit_bytes=VMEM_LIMIT),
        cost_estimate=pl.CostEstimate(flops=flops, bytes_accessed=1, transcendentals=0),
    )()


def split(value):
    high = value.astype(jnp.bfloat16)
    low = (value - high.astype(jnp.float32)).astype(jnp.bfloat16)
    return high, low


def find(owner, target):
    found = []
    for slot in range(CAP):
        seen, index, filled = jnp.int32(0), jnp.int32(0), jnp.int32(0)
        for k in range(owner.shape[0]):
            match = owner[k] == target
            hit = jnp.logical_and(match, seen == slot)
            index = jnp.where(hit, k, index)
            filled = jnp.where(hit, 1, filled)
            seen = seen + match.astype(jnp.int32)
        found.append((index, filled))
    return found


def exchange(value, axis, distance):
    size = lax.axis_size(axis)
    return lax.ppermute(value, axis, [(i, i ^ distance) for i in range(size)])


def pick_kernel(integrals, *rest):
    *pieces, sems = rest
    here = lax.axis_index("tiles")
    copies = []
    for distance, piece in enumerate(pieces):
        start = pl.multiple_of((here ^ distance) * PAIR, PAIR)
        copies.append(pltpu.make_async_copy(integrals.at[:, pl.ds(start, PAIR)], piece, sems.at[distance]))
    for copy in copies:
        copy.start()
    for copy in copies:
        copy.wait()


def split_kernel(stored, high, low):
    value_high, value_low = split(stored[...])
    high[...] = value_high
    low[...] = value_low


def partial_kernel(distance, owner, piece, high, low, send, own):
    rows = own.shape[0]
    target = lax.axis_index("tiles") ^ distance
    rep = lax.axis_index("rep")
    (first, has_first), (second, has_second) = find(owner, target)
    lane = lax.broadcasted_iota(jnp.int32, (rows, PAIR), 1)
    kept = jnp.where(lane < TILE, has_first, has_second) == 1
    right_high = jnp.concatenate([high[first], high[second]], axis=0)
    right_low = jnp.concatenate([low[first], low[second]], axis=0)
    parts = []
    for pair_of in (1 - rep, rep):
        block = piece[pl.ds(pl.multiple_of(pair_of * rows, rows), rows), :]
        parts.append(jnp.where(kept, block, 0.0))
    left_high, left_low = split(jnp.concatenate(parts, axis=0))
    dot = functools.partial(jnp.dot, preferred_element_type=jnp.float32)
    product = dot(left_high, right_high) + (dot(left_high, right_low) + dot(left_low, right_high))
    send[...] = product[:rows]
    own[...] = product[rows:]


def square_shards(amplitudes, integrals, tile_owner):
    groups = lax.axis_size("tiles")
    stored = amplitudes.reshape(amplitudes.shape[2:])
    owner = tile_owner.reshape(tile_owner.shape[2])
    rows = integrals.shape[1]
    matrix = integrals.reshape(-1, integrals.shape[3])
    columns = stored.shape[2]

    picked = call(
        pick_kernel,
        [f32(matrix.shape[0], PAIR)] * groups,
        [ANY],
        [pltpu.SemaphoreType.DMA((groups,))],
        10**10,
    )(matrix)
    pieces = [picked[0]] + [exchange(picked[e], "tiles", e) for e in range(1, groups)]
    half = jax.ShapeDtypeStruct(stored.shape, jnp.bfloat16)
    high, low = pl.pallas_call(
        split_kernel,
        out_shape=[half, half],
        grid=(stored.shape[0],),
        in_specs=[pl.BlockSpec((1,) + stored.shape[1:], lambda k: (k, 0, 0))],
        out_specs=[pl.BlockSpec((1,) + stored.shape[1:], lambda k: (k, 0, 0))] * 2,
        compiler_params=pltpu.CompilerParams(vmem_limit_bytes=VMEM_LIMIT),
        cost_estimate=pl.CostEstimate(flops=1, bytes_accessed=1, transcendentals=0),
    )(stored)

    sums = {}
    for e in (1, 3, 2, 0):
        send, own = call(functools.partial(partial_kernel, e), [f32(rows, columns)] * 2, [SMEM] + [VMEM] * 3)(
            owner, pieces[e], high, low
        )
        sums[e] = own + exchange(send, "rep", 1)
    out = sums[0]
    for e in (1, 3, 2):
        out = out + exchange(sums[e], "tiles", e)
    return out.reshape(1, rows, columns)


def general_shards(amplitudes, integrals, tile_owner):
    tile_groups = lax.axis_size("tiles")
    stored = amplitudes.reshape(amplitudes.shape[2:])
    owners = tile_owner.reshape(tile_owner.shape[2])
    earlier = jnp.arange(owners.shape[0])[:, None] > jnp.arange(owners.shape[0])[None, :]
    matching = owners[:, None] == owners[None, :]
    slot_index = owners * CAP + jnp.sum(matching & earlier, axis=1)
    out_tiles, tile_rows, _, inner_width = integrals.shape
    columns = stored.shape[2]
    matrix = integrals.reshape(out_tiles * tile_rows, inner_width)
    outgoing = jnp.zeros((tile_groups * CAP, TILE, columns), jnp.float32).at[slot_index].set(stored)
    outgoing = outgoing.reshape(tile_groups, CAP, TILE, columns)
    received = lax.all_to_all(outgoing, "tiles", split_axis=0, concat_axis=0, tiled=True)
    product = jnp.dot(
        matrix, received.reshape(inner_width, columns), precision=lax.Precision.HIGHEST, preferred_element_type=jnp.float32
    )
    partial_value = product.reshape(out_tiles, tile_rows, columns)
    return lax.psum_scatter(partial_value, "rep", scatter_dimension=0, tiled=True)


def solution(mesh):
    small = mesh.shape["tiles"] == 4 and mesh.shape["rep"] == 2
    return jax.shard_map(
        square_shards if small else general_shards,
        mesh=mesh,
        in_specs=(
            P(("groups", "tiles"), "rep", None, None, None),
            P(("groups", "tiles"), "sub", "rep", None),
            P(("groups", "tiles"), "rep", None),
        ),
        out_specs=P(("groups", "tiles", "rep"), "sub", None),
        check_vma=False,
    )
```

```python
import functools

import jax
import jax.numpy as jnp
from jax import lax
from jax.experimental import pallas as pl
from jax.experimental.pallas import tpu as pltpu
from jax.sharding import PartitionSpec as P

TILE = 64
CAP = 2
EARLY = {2: 512, 1: 896}
COST = {'f0': 10, 'f1': 5, 'f2': 1, 'k3': 5, 'k1': 5}
AFTER = {'a2': (('fold', 2),), 'fold1': (('s', 3),), 'a1': (('s', 3),)}
PAIR = TILE * CAP
VMEM_LIMIT = 32 * 1024 * 1024
ANY = pl.BlockSpec(memory_space=pl.ANY)
VMEM = pl.BlockSpec(memory_space=pltpu.VMEM)
SMEM = pl.BlockSpec(memory_space=pltpu.SMEM)


def f32(*shape):
    return jax.ShapeDtypeStruct(shape, jnp.float32)


def call(kernel, outs, ins, scratch=(), flops=1):
    return functools.partial(
        pl.pallas_call,
        kernel,
        out_shape=outs,
        in_specs=ins,
        out_specs=jax.tree.map(lambda _: VMEM, outs),
        scratch_shapes=list(scratch),
        compiler_params=pltpu.CompilerParams(vmem_limit_bytes=VMEM_LIMIT),
        cost_estimate=pl.CostEstimate(flops=flops, bytes_accessed=1, transcendentals=0),
    )()


def split(value):
    high = value.astype(jnp.bfloat16)
    low = (value - high.astype(jnp.float32)).astype(jnp.bfloat16)
    return high, low


def find(owner, target):
    found = []
    for slot in range(CAP):
        seen, index, filled = jnp.int32(0), jnp.int32(0), jnp.int32(0)
        for k in range(owner.shape[0]):
            match = owner[k] == target
            hit = jnp.logical_and(match, seen == slot)
            index = jnp.where(hit, k, index)
            filled = jnp.where(hit, 1, filled)
            seen = seen + match.astype(jnp.int32)
        found.append((index, filled))
    return found


def exchange(value, axis, distance):
    size = lax.axis_size(axis)
    return lax.ppermute(value, axis, [(i, i ^ distance) for i in range(size)])


def pick_kernel(integrals, *rest):
    *pieces, sems = rest
    here = lax.axis_index("tiles")
    copies = []
    for distance, piece in enumerate(pieces):
        start = pl.multiple_of((here ^ distance) * PAIR, PAIR)
        copies.append(pltpu.make_async_copy(integrals.at[:, pl.ds(start, PAIR)], piece, sems.at[distance]))
    for copy in copies:
        copy.start()
    for copy in copies:
        copy.wait()


def split_kernel(stored, high, low):
    value_high, value_low = split(stored[...])
    high[...] = value_high
    low[...] = value_low


def ordered(piece):
    rows = piece.shape[0] // 2
    rep = lax.axis_index("rep")
    return jnp.concatenate([piece[pl.ds(pl.multiple_of(q * rows, rows), rows), :] for q in (1 - rep, rep)], axis=0)


def doubled(value):
    high, low = split(value)
    return jnp.concatenate(
        [jnp.concatenate([high, high], axis=1), jnp.concatenate([low, jnp.zeros_like(low)], axis=1)], axis=0
    )


def multiply(distance, owner, piece, high, low, start):
    found = find(owner, lax.axis_index("tiles") ^ distance)
    lane = lax.broadcasted_iota(jnp.int32, piece.shape, 1)
    kept = jnp.where(lane < TILE, found[0][1], found[1][1]) == 1
    left = doubled(jnp.where(kept, ordered(piece), 0.0))
    right = jnp.concatenate([half[k, :, start:] for half in (high, low) for k, _ in found], axis=0)
    product = jnp.dot(left, right, preferred_element_type=jnp.float32)
    return product[: piece.shape[0]] + product[piece.shape[0] :]


def partial_kernel(distance, owner, piece, high, low, *rest):
    send, own = rest[0], rest[1]
    rows = own.shape[0]
    product = multiply(distance, owner, piece, high, low, 0)
    cut = product.shape[1] - own.shape[1]
    send[...] = product[:rows, cut:]
    own[...] = product[rows:, cut:]
    if cut:
        rest[2][...] = product[:, :cut]


def fold_kernel(send, own, early, *rest):
    send_out, own_out = rest[-2:]
    rows, width = own.shape[0], early.shape[1]
    send_out[...] = send[...]
    own_out[...] = own[...]
    send_out[:, :width] += early[:rows]
    own_out[:, :width] += early[rows:]


def add_kernel(first, *rest):
    *others, out = rest
    out[...] = first[...]
    for other in others:
        skip = out.shape[1] - other.shape[1]
        out[:, skip:] += other[...]


def square_shards(amplitudes, integrals, tile_owner):
    groups = lax.axis_size("tiles")
    stored = amplitudes.reshape(amplitudes.shape[2:])
    owner = tile_owner.reshape(tile_owner.shape[2])
    rows = integrals.shape[1]
    matrix = integrals.reshape(-1, integrals.shape[3])
    columns = stored.shape[2]

    picked = call(
        pick_kernel,
        [f32(matrix.shape[0], PAIR)] * groups,
        [ANY],
        [pltpu.SemaphoreType.DMA((groups,))],
        10**10,
    )(matrix)
    pieces = [picked[0]] + [exchange(picked[e], "tiles", e) for e in range(1, groups)]
    half = jax.ShapeDtypeStruct(stored.shape, jnp.bfloat16)
    high, low = pl.pallas_call(
        split_kernel,
        out_shape=[half, half],
        grid=(stored.shape[0],),
        in_specs=[pl.BlockSpec((1,) + stored.shape[1:], lambda k: (k, 0, 0))],
        out_specs=[pl.BlockSpec((1,) + stored.shape[1:], lambda k: (k, 0, 0))] * 2,
        compiler_params=pltpu.CompilerParams(vmem_limit_bytes=VMEM_LIMIT),
        cost_estimate=pl.CostEstimate(flops=1, bytes_accessed=1, transcendentals=0),
    )(stored)

    def kernel(name, body, outs, ins, args, after=()):
        waits = [everything[key] for key in after]

        def run(*refs):
            body(*refs[: len(args)], *refs[len(args) + len(waits) :])

        return call(run, outs, ins + [ANY] * len(waits), (), int(COST.get(name, 0) * 1.15e9) + 1)(*args, *waits)

    everything = {("j", e): pieces[e] for e in range(groups)}
    def partial(e):
        cut = EARLY.get(e, 0)
        shapes = [f32(rows, columns - cut)] * 2 + ([f32(2 * rows, cut)] if cut else [])
        waits = AFTER.get(e, ())
        send, own, *more = kernel(
            f"k{e}", functools.partial(partial_kernel, e), shapes, [SMEM] + [VMEM] * 3,
            [owner, pieces[e], high, low], waits,
        )
        everything["k", e] = own
        if more:
            early[e] = exchange(more[0], "tiles", e)
        return (send, own) if e == 0 else (exchange(send, "rep", 1), own)

    def finish(e, arrived, own):
        (total,) = kernel(f"a{e}", add_kernel, [f32(*own.shape)], [VMEM] * 2, [own, arrived], AFTER.get(f"a{e}", ()))
        everything["s", e] = total
        return exchange(total, "tiles", e)

    early = {}
    parts = {e: partial(e) for e in (1, 3, 2, 0)}
    send, own = parts[0]
    got = {}
    for step in (2, -2, -3, 1, -1):
        if step in early:
            send, own = kernel(
                f"fold{step}", fold_kernel, [f32(rows, columns)] * 2, [VMEM] * 3, [send, own, early[step]], AFTER.get(f"fold{step}", ())
            )
            everything["fold", step] = own
        else:
            got[-step] = finish(-step, *parts[-step])
    got[0] = exchange(send, "rep", 1)
    out = own
    for n, group in enumerate(((2,), (3,), (1, 0))):
        (out,) = kernel(f"f{n}", add_kernel, [f32(rows, columns)], [VMEM] * (1 + len(group)), [out] + [got[e] for e in group])
    return out.reshape(1, rows, columns)


def general_shards(amplitudes, integrals, tile_owner):
    tile_groups = lax.axis_size("tiles")
    stored = amplitudes.reshape(amplitudes.shape[2:])
    owners = tile_owner.reshape(tile_owner.shape[2])
    earlier = jnp.arange(owners.shape[0])[:, None] > jnp.arange(owners.shape[0])[None, :]
    matching = owners[:, None] == owners[None, :]
    slot_index = owners * CAP + jnp.sum(matching & earlier, axis=1)
    out_tiles, tile_rows, _, inner_width = integrals.shape
    columns = stored.shape[2]
    matrix = integrals.reshape(out_tiles * tile_rows, inner_width)
    outgoing = jnp.zeros((tile_groups * CAP, TILE, columns), jnp.float32).at[slot_index].set(stored)
    outgoing = outgoing.reshape(tile_groups, CAP, TILE, columns)
    received = lax.all_to_all(outgoing, "tiles", split_axis=0, concat_axis=0, tiled=True)
    product = jnp.dot(
        matrix, received.reshape(inner_width, columns), precision=lax.Precision.HIGHEST, preferred_element_type=jnp.float32
    )
    partial_value = product.reshape(out_tiles, tile_rows, columns)
    return lax.psum_scatter(partial_value, "rep", scatter_dimension=0, tiled=True)


def solution(mesh):
    small = mesh.shape["tiles"] == 4 and mesh.shape["rep"] == 2
    return jax.shard_map(
        square_shards if small else general_shards,
        mesh=mesh,
        in_specs=(
            P(("groups", "tiles"), "rep", None, None, None),
            P(("groups", "tiles"), "sub", "rep", None),
            P(("groups", "tiles"), "rep", None),
        ),
        out_specs=P(("groups", "tiles", "rep"), "sub", None),
        check_vma=False,
    )
```

```python
import functools

import jax
import jax.numpy as jnp
from jax import lax
from jax.experimental import pallas as pl
from jax.experimental.pallas import tpu as pltpu
from jax.sharding import PartitionSpec as P

TILE = 64
CAP = 2
EARLY = {2: 512, 1: 896}
COST = {'f0': 10, 'f1': 5, 'f2': 1, 'k3': 5, 'k1': 0}
AFTER = {'a2': (('fold', 2),), 'fold1': (('s', 3),), 'a1': (('s', 3),)}
APART = (2,)
PAIR = TILE * CAP
VMEM_LIMIT = 32 * 1024 * 1024
ANY = pl.BlockSpec(memory_space=pl.ANY)
VMEM = pl.BlockSpec(memory_space=pltpu.VMEM)
SMEM = pl.BlockSpec(memory_space=pltpu.SMEM)


def f32(*shape):
    return jax.ShapeDtypeStruct(shape, jnp.float32)


def call(kernel, outs, ins, scratch=(), flops=1):
    return functools.partial(
        pl.pallas_call,
        kernel,
        out_shape=outs,
        in_specs=ins,
        out_specs=jax.tree.map(lambda _: VMEM, outs),
        scratch_shapes=list(scratch),
        compiler_params=pltpu.CompilerParams(vmem_limit_bytes=VMEM_LIMIT),
        cost_estimate=pl.CostEstimate(flops=flops, bytes_accessed=1, transcendentals=0),
    )()


def split(value):
    high = value.astype(jnp.bfloat16)
    low = (value - high.astype(jnp.float32)).astype(jnp.bfloat16)
    return high, low


def find(owner, target):
    found = []
    for slot in range(CAP):
        seen, index, filled = jnp.int32(0), jnp.int32(0), jnp.int32(0)
        for k in range(owner.shape[0]):
            match = owner[k] == target
            hit = jnp.logical_and(match, seen == slot)
            index = jnp.where(hit, k, index)
            filled = jnp.where(hit, 1, filled)
            seen = seen + match.astype(jnp.int32)
        found.append((index, filled))
    return found


def exchange(value, axis, distance):
    size = lax.axis_size(axis)
    return lax.ppermute(value, axis, [(i, i ^ distance) for i in range(size)])


def pick_kernel(integrals, *rest):
    *pieces, sems = rest
    here = lax.axis_index("tiles")
    copies = []
    for distance, piece in enumerate(pieces):
        start = pl.multiple_of((here ^ distance) * PAIR, PAIR)
        copies.append(pltpu.make_async_copy(integrals.at[:, pl.ds(start, PAIR)], piece, sems.at[distance]))
    for copy in copies:
        copy.start()
    for copy in copies:
        copy.wait()


def split_kernel(stored, high, low):
    value_high, value_low = split(stored[...])
    high[...] = value_high
    low[...] = value_low


def ordered(piece):
    rows = piece.shape[0] // 2
    rep = lax.axis_index("rep")
    return jnp.concatenate([piece[pl.ds(pl.multiple_of(q * rows, rows), rows), :] for q in (1 - rep, rep)], axis=0)


def doubled(value):
    high, low = split(value)
    return jnp.concatenate(
        [jnp.concatenate([high, high], axis=1), jnp.concatenate([low, jnp.zeros_like(low)], axis=1)], axis=0
    )


def sort_kernel(owner, stored, tiles):
    here = lax.axis_index("tiles")
    for distance in range(tiles.shape[0]):
        for slot, (index, filled) in enumerate(find(owner, here ^ distance)):
            tile = stored[index]
            high, low = split(jnp.where(filled == 1, tile, jnp.zeros_like(tile)))
            tiles[distance, slot * TILE : (slot + 1) * TILE, :] = high
            tiles[distance, PAIR + slot * TILE : PAIR + (slot + 1) * TILE, :] = low


def partial_kernel(distance, piece, tiles, *rest):
    send, own = rest[0], rest[1]
    rows = own.shape[0]
    product = jnp.dot(doubled(ordered(piece)), tiles[distance], preferred_element_type=jnp.float32)
    product = product[: 2 * rows] + product[2 * rows :]
    cut = product.shape[1] - own.shape[1]
    send[...] = product[:rows, cut:]
    own[...] = product[rows:, cut:]
    if cut:
        rest[2][...] = product[:, :cut]


def fold_kernel(send, own, early, *rest):
    send_out, own_out = rest[-2:]
    rows, width = own.shape[0], early.shape[1]
    send_out[...] = send[...]
    own_out[...] = own[...]
    send_out[:, :width] += early[:rows]
    own_out[:, :width] += early[rows:]


def add_kernel(first, *rest):
    *others, out = rest
    out[...] = first[...]
    for other in others:
        skip = out.shape[1] - other.shape[1]
        out[:, skip:] += other[...]


def square_shards(amplitudes, integrals, tile_owner):
    groups = lax.axis_size("tiles")
    stored = amplitudes.reshape(amplitudes.shape[2:])
    owner = tile_owner.reshape(tile_owner.shape[2])
    rows = integrals.shape[1]
    matrix = integrals.reshape(-1, integrals.shape[3])
    columns = stored.shape[2]

    picked = call(
        pick_kernel,
        [f32(matrix.shape[0], PAIR)] * groups,
        [ANY],
        [pltpu.SemaphoreType.DMA((groups,))],
        10**10,
    )(matrix)
    pieces = [picked[0]] + [exchange(picked[e], "tiles", e) for e in range(1, groups)]
    (tiles,) = call(
        sort_kernel,
        [jax.ShapeDtypeStruct((groups, 2 * PAIR, columns), jnp.bfloat16)],
        [SMEM, VMEM],
    )(owner, stored)

    def kernel(name, body, outs, ins, args, after=()):
        waits = [everything[key] for key in after]

        def run(*refs):
            body(*refs[: len(args)], *refs[len(args) + len(waits) :])

        return call(run, outs, ins + [ANY] * len(waits), (), int(COST.get(name, 0) * 1.15e9) + 1)(*args, *waits)

    everything = {("j", e): pieces[e] for e in range(groups)}
    def partial(e):
        cut = EARLY.get(e, 0)
        shapes = [f32(rows, columns - cut)] * 2 + ([f32(2 * rows, cut)] if cut else [])
        waits = AFTER.get(e, ())
        send, own, *more = kernel(
            f"k{e}", functools.partial(partial_kernel, e), shapes, [VMEM] * 2,
            [pieces[e], tiles], waits,
        )
        everything["k", e] = own
        if more:
            early[e] = exchange(more[0], "tiles", e)
        return (send, own) if e == 0 else (exchange(send, "rep", 1), own)

    def finish(e, arrived, own):
        (total,) = kernel(f"a{e}", add_kernel, [f32(*own.shape)], [VMEM] * 2, [own, arrived], AFTER.get(f"a{e}", ()))
        everything["s", e] = total
        return exchange(total, "tiles", e)

    early = {}
    parts = {e: partial(e) for e in (1, 3, 2, 0)}
    send, own = parts[0]
    got = {}
    for step in (2, -2, -3, 1, -1):
        if step in early:
            send, own = kernel(
                f"fold{step}", fold_kernel, [f32(rows, columns)] * 2, [VMEM] * 3, [send, own, early[step]], AFTER.get(f"fold{step}", ())
            )
            everything["fold", step] = own
        else:
            got[-step] = finish(-step, *parts[-step])
    got[0] = exchange(send, "rep", 1)
    out = own
    for n, group in enumerate(((2,), (3,), (1, 0))):
        (out,) = kernel(f"f{n}", add_kernel, [f32(rows, columns)], [VMEM] * (1 + len(group)), [out] + [got[e] for e in group])
    return out.reshape(1, rows, columns)


def general_shards(amplitudes, integrals, tile_owner):
    tile_groups = lax.axis_size("tiles")
    stored = amplitudes.reshape(amplitudes.shape[2:])
    owners = tile_owner.reshape(tile_owner.shape[2])
    earlier = jnp.arange(owners.shape[0])[:, None] > jnp.arange(owners.shape[0])[None, :]
    matching = owners[:, None] == owners[None, :]
    slot_index = owners * CAP + jnp.sum(matching & earlier, axis=1)
    out_tiles, tile_rows, _, inner_width = integrals.shape
    columns = stored.shape[2]
    matrix = integrals.reshape(out_tiles * tile_rows, inner_width)
    outgoing = jnp.zeros((tile_groups * CAP, TILE, columns), jnp.float32).at[slot_index].set(stored)
    outgoing = outgoing.reshape(tile_groups, CAP, TILE, columns)
    received = lax.all_to_all(outgoing, "tiles", split_axis=0, concat_axis=0, tiled=True)
    product = jnp.dot(
        matrix, received.reshape(inner_width, columns), precision=lax.Precision.HIGHEST, preferred_element_type=jnp.float32
    )
    partial_value = product.reshape(out_tiles, tile_rows, columns)
    return lax.psum_scatter(partial_value, "rep", scatter_dimension=0, tiled=True)


def solution(mesh):
    small = mesh.shape["tiles"] == 4 and mesh.shape["rep"] == 2
    return jax.shard_map(
        square_shards if small else general_shards,
        mesh=mesh,
        in_specs=(
            P(("groups", "tiles"), "rep", None, None, None),
            P(("groups", "tiles"), "sub", "rep", None),
            P(("groups", "tiles"), "rep", None),
        ),
        out_specs=P(("groups", "tiles", "rep"), "sub", None),
        check_vma=False,
    )
```
